32 devices in a mesh: rep: 2 (over y), seq: 4 (over z), head: 4 (over x, core).
Axes of the slice: x: 2, y: 2, z: 4, core: 2. Of those that a mesh axis runs over, the one named last changes fastest.
Arguments:
- queries: bfloat16 [4096, 1024], P(('rep', 'seq', 'head')), parts along dimension 0, may hold values from -6 to 6
- keys: bfloat16 [4096, 2, 1024], P(('rep', 'seq', 'head')), parts along dimension 0, may hold values from -6 to 6
- values: bfloat16 [4096, 2, 1024], P(('rep', 'seq', 'head')), parts along dimension 0, may hold values from -6 to 6
- out_gate: bfloat16 [4096, 1024], P(('rep', 'seq', 'head')), parts along dimension 0, may hold values from -6 to 6
- write_rate: bfloat16 [4096, 2, 8], P(('rep', 'seq', 'head')), parts along dimension 0, may hold values from 0 to 2
- log_decay: bfloat16 [4096, 8], P(('rep', 'seq', 'head')), parts along dimension 0, may hold values from -0.7 to 0
- doc_starts: int32 [8], P('rep'), parts along dimension 0, may hold values from 0 to 2047, as said below
- norm_gain: float32 [128], replicated, may hold values from 0.1 to 1.9
- out_weight: bfloat16 [1024, 2048], P(None, 'head'), may hold values from -0.1875 to 0.1875
Outputs:
- layer_out: bfloat16 [4096, 2048], P(('rep', 'seq'), 'head'), parts along dimension 0
The draws below stay inside these ranges and needn't reach their ends.
There are 2 independent parts, one for each index of `rep`. The reference program is written for one: setup_inputs(seed, part) draws one part's arguments, and reference() takes and returns one part's arrays. A program takes and returns all parts, laid end to end along the dimension named above; an argument that names none is the same for every part. Nothing has to cross between parts.
Inputs may be any that keep to these rules, and one draw needn't show every extreme that they name: `doc_starts`: rises strictly from 0; one document holds exactly 1024 tokens, every other fewer, each at least one.
All inputs are finite; a program needn't handle non-finite values.
Results may differ from the reference program's by a relative error of at most 0.007.
Values may be sent and summed in bfloat16 or wider, within the bound.
A program may use at most 64 MiB of HBM per device.

```python
import math
import jax
import jax.numpy as jnp
from jax import lax

D = 2048
HEAD_TOTAL = 8
DK = 128
PACKED_TOKENS = 2048
DOCS = 4


def head_varieties(key):
    base_key = jax.random.fold_in(key, 7)
    random_subkeys = jax.random.split(base_key, 6)
    fast_count = jax.random.randint(random_subkeys[0], (), HEAD_TOTAL // 4, HEAD_TOTAL // 2 + 1)
    ranking = jax.random.permutation(random_subkeys[1], HEAD_TOTAL)
    head_is_quick = ranking < fast_count
    quick_write_rate = jnp.exp(jax.random.uniform(random_subkeys[2], (HEAD_TOTAL,), jnp.float32, math.log(1.0 / 50.0), math.log(1.0 / 30.0)))
    gentle_write_rate = jnp.exp(jax.random.uniform(random_subkeys[3], (HEAD_TOTAL,), jnp.float32, math.log(0.05), math.log(0.2))) / PACKED_TOKENS
    gentle_update = 64.0 * jnp.exp(jax.random.uniform(random_subkeys[4], (HEAD_TOTAL,), jnp.float32, math.log(0.1), math.log(0.5))) / PACKED_TOKENS
    write_groups = jax.random.randint(random_subkeys[5], (2, HEAD_TOTAL), 0, PACKED_TOKENS)
    return (head_is_quick, quick_write_rate, gentle_write_rate, gentle_update, write_groups)


def rough_factor(key, shape):
    return jnp.exp(jax.random.uniform(key, shape, jnp.float32, math.log(0.5), math.log(2.0)))


def draw_log_decay(key, part):
    head_is_quick, quick_write_rate, gentle_write_rate, gentle_update, write_groups = head_varieties(key)
    rough = rough_factor(jax.random.fold_in(key, 11), (PACKED_TOKENS, HEAD_TOTAL))
    decay_logs = -jnp.where(head_is_quick, quick_write_rate, gentle_write_rate)[None, :] * rough
    token_position = jnp.arange(PACKED_TOKENS, dtype=jnp.int32)[:, None]
    reset_state = (token_position == write_groups[0][None, :]) | (token_position == write_groups[1][None, :])
    dropped = jax.random.uniform(jax.random.fold_in(key, 13), (PACKED_TOKENS, HEAD_TOTAL), jnp.float32, 0.5, 0.8)
    decay_logs = jnp.where(reset_state, jnp.log(dropped), decay_logs)
    return decay_logs.astype(jnp.bfloat16)


def draw_write_rate(key, part):
    head_is_quick, quick_write_rate, gentle_write_rate, gentle_update, write_groups = head_varieties(key)
    fast_beta = jax.random.uniform(jax.random.fold_in(key, 17), (PACKED_TOKENS, 2, HEAD_TOTAL), jnp.float32, 0.2, 1.9)
    slow_beta = gentle_update[None, None, :] * rough_factor(jax.random.fold_in(key, 19), (PACKED_TOKENS, 2, HEAD_TOTAL))
    return jnp.where(head_is_quick[None, None, :], fast_beta, slow_beta).astype(jnp.bfloat16)


def draw_doc_starts(key, part):
    random_subkeys = jax.random.split(jax.random.fold_in(key, 3), 2)
    longest = PACKED_TOKENS // 2
    remain = PACKED_TOKENS - longest
    shuffled = jax.random.permutation(random_subkeys[0], remain - 1) + 1
    cut_points = jnp.sort(shuffled[:DOCS - 2]).astype(jnp.int32)
    bounds = jnp.concatenate([jnp.zeros((1,), jnp.int32), cut_points, jnp.full((1,), remain, jnp.int32)])
    shorts = bounds[1:] - bounds[:-1]
    placed = jax.random.randint(random_subkeys[1], (), 0, DOCS)
    slot_ids = jnp.arange(DOCS, dtype=jnp.int32)
    source = jnp.clip(jnp.where(slot_ids < placed, slot_ids, slot_ids - 1), 0, DOCS - 2)
    lengths = jnp.where(slot_ids == placed, longest, shorts[source]).astype(jnp.int32)
    return (jnp.cumsum(lengths) - lengths).astype(jnp.int32)


def block_levels(stream_key, shape, pieces, least, high):
    gain, own = 1.0, jax.random.fold_in(stream_key, 6)
    for axis_at, parts in pieces:
        heights = jnp.exp(jax.random.uniform(jax.random.fold_in(own, axis_at), (parts,), jnp.float32, least / len(pieces), high / len(pieces)))
        gain = gain * jnp.repeat(heights, shape[axis_at] // parts).reshape([-1 if axis == axis_at else 1 for axis in range(len(shape))])
    return gain


def bell_draw(own_key, dims, spread, bound, shards=(), kind=jnp.bfloat16):
    values = spread * jax.random.normal(own_key, dims, jnp.float32)
    if shards:
        values = values * block_levels(own_key, dims, shards, -0.22, 0.18)
    return jnp.clip(values, -bound, bound).astype(kind)


def setup_inputs(seed: int = 0, part: int = 0) -> dict:
    seeds = jax.random.split(jax.random.key(seed), 10)
    part_splits = jax.random.split(jax.random.fold_in(seeds[9], part), 10)
    return {
        "queries": bell_draw(part_splits[0], (PACKED_TOKENS, HEAD_TOTAL * DK), 1.0, 6.0, ((0, 16),)),
        "keys": bell_draw(part_splits[1], (PACKED_TOKENS, 2, HEAD_TOTAL * DK), 1.0, 6.0, ((0, 16),)),
        "values": bell_draw(part_splits[2], (PACKED_TOKENS, 2, HEAD_TOTAL * DK), 1.0, 6.0, ((0, 16),)),
        "out_gate": bell_draw(part_splits[3], (PACKED_TOKENS, HEAD_TOTAL * DK), 1.0, 6.0, ((0, 16),)),
        "write_rate": draw_write_rate(jax.random.fold_in(jax.random.fold_in(seeds[9], part), 71), part),
        "log_decay": draw_log_decay(jax.random.fold_in(jax.random.fold_in(seeds[9], part), 71), part),
        "doc_starts": draw_doc_starts(jax.random.fold_in(jax.random.fold_in(seeds[9], part), 71), part),
        "norm_gain": jnp.clip(1.0 + 0.18 * jax.random.normal(seeds[7], (DK,), jnp.float32), 0.1, 1.9),
        "out_weight": bell_draw(seeds[8], (HEAD_TOTAL * DK, D), (HEAD_TOTAL * DK) ** -0.5, 0.1875, ((1, 4),)),
    }


PRECISE_SETTING = lax.Precision.HIGHEST

def reference(queries, keys, values, out_gate, write_rate, log_decay, doc_starts, norm_gain, out_weight):
    positions = jnp.arange(PACKED_TOKENS, dtype=jnp.int32)
    begins = lax.optimization_barrier(jnp.sum((positions[:, None] == doc_starts[None, :]).astype(jnp.int32), 1)) > 0
    decay_rate = jnp.where(begins[:, None], jnp.float32(0.0), jnp.exp(log_decay.astype(jnp.float32)))
    unit_keys = keys.astype(jnp.float32).reshape(PACKED_TOKENS, 2, HEAD_TOTAL, DK)
    unit_keys = unit_keys / jnp.sqrt(lax.optimization_barrier(jnp.sum(unit_keys * unit_keys, -1, keepdims=True)) + 1e-06)
    value_rows = values.astype(jnp.float32).reshape(PACKED_TOKENS, 2, HEAD_TOTAL, DK)
    write_rates = write_rate.astype(jnp.float32)
    query_rows = queries.astype(jnp.float32).reshape(PACKED_TOKENS, HEAD_TOTAL, DK)

    def advance(current_state, inputs):
        fade_now, current_key, value_now, rate_now, current_query = inputs
        current_state = fade_now[:, None, None] * current_state
        for reflector_update in range(2):
            state_readout = jnp.einsum('bf,bft->bt', current_key[reflector_update], current_state, precision=PRECISE_SETTING)
            change = (value_now[reflector_update] - state_readout)[:, None, :]
            current_state = current_state + rate_now[reflector_update][:, None, None] * current_key[reflector_update][:, :, None] * change
        return (current_state, jnp.einsum('bf,bft->bt', current_query, current_state, precision=PRECISE_SETTING))
    zero_state = jnp.zeros((HEAD_TOTAL, DK, DK), jnp.float32)
    final_state, readout = lax.scan(advance, zero_state, (decay_rate, unit_keys, value_rows, write_rates, query_rows))
    gate_vals = out_gate.astype(jnp.float32).reshape(PACKED_TOKENS, HEAD_TOTAL, DK)
    inv_rms = lax.rsqrt(lax.optimization_barrier(jnp.mean(readout * readout, -1, keepdims=True)) + 1e-05)
    normed = (readout * inv_rms * norm_gain * jax.nn.silu(gate_vals)).astype(jnp.bfloat16)
    normed = normed.reshape(PACKED_TOKENS, HEAD_TOTAL * DK)
    return jnp.dot(normed, out_weight, preferred_element_type=jnp.float32).astype(jnp.bfloat16)
```

```python
import functools

import jax
import jax.numpy as jnp
from jax import lax
from jax.experimental import pallas as pl
from jax.experimental.pallas import tpu as pltpu
from jax.sharding import PartitionSpec as P

F32 = jnp.float32
BF16 = jnp.bfloat16


def mm(a, b):
    return jnp.dot(a.astype(BF16), b.astype(BF16), preferred_element_type=F32)


def mm_nt(a, b):
    return lax.dot_general(
        a.astype(BF16), b.astype(BF16), (((1,), (1,)), ((), ())), preferred_element_type=F32
    )


def mm_tn(a, b):
    return lax.dot_general(
        a.astype(BF16), b.astype(BF16), (((0,), (0,)), ((), ())), preferred_element_type=F32
    )


def iota(shape, dim):
    return lax.broadcasted_iota(jnp.int32, shape, dim)


def unit_lower_inverse(parts, half):
    rows, cols = iota((half, half), 0), iota((half, half), 1)
    size = 1
    inverses = None
    while size < half:
        row_block, col_block = rows // size, cols // size
        link = (row_block == col_block + 1) & (row_block % 2 == 1)
        linked = [jnp.where(link, part, 0.0) for part in parts]
        if inverses is None:
            eye = jnp.where(rows == cols, 1.0, 0.0)
            inverses = [eye - part for part in linked]
        else:
            short = [inverse.astype(BF16) for inverse in inverses]
            middle = [mm(part, inverse) for part, inverse in zip(linked, short)]
            fixes = [mm(inverse, part) for inverse, part in zip(short, middle)]
            inverses = [inverse - fix for inverse, fix in zip(inverses, fixes)]
        size *= 2
    return inverses


def piece_kernel(
    doc_ref,
    query_ref,
    key_ref,
    value_ref,
    rate_ref,
    decay_ref,
    inner_ref,
    carried_ref,
    state_ref,
    *,
    heads_step,
    head_depth,
):
    tokens = query_ref.shape[0]
    steps = 2 * tokens
    half = steps // 2
    heads_all = rate_ref.shape[1]
    docs = doc_ref.shape[0]
    first = (lax.axis_index("seq") * lax.axis_size("head") + lax.axis_index("head")) * tokens

    def doc_of(position):
        return sum((position >= doc_ref[index]).astype(jnp.int32) for index in range(docs))

    doc_before = doc_of(first - 1)
    doc_last = doc_of(first + tokens - 1)
    step_doc_col = doc_of(first + iota((steps, half), 0) // 2)
    step_doc_row = doc_of(first + iota((1, steps), 1) // 2)
    token_doc_col = doc_of(first + iota((tokens, steps), 0))
    col_ids = iota((tokens, steps), 1)
    score_mask = (col_ids <= 2 * iota((tokens, steps), 0) + 1) & (token_doc_col == step_doc_row)
    step_tri = (iota((steps, tokens), 1) <= iota((steps, tokens), 0) // 2).astype(BF16)
    token_tri = (iota((tokens, tokens), 1) <= iota((tokens, tokens), 0)).astype(BF16)
    row_tri = (iota((tokens, steps), 0) <= iota((tokens, steps), 1) // 2).astype(BF16)
    rows, cols = iota((half, half), 0), iota((half, half), 1)
    eye = rows == cols
    lower = rows > cols
    docs_low = step_doc_col[half:] == step_doc_row[:, :half]
    docs_first = (step_doc_col[:half] == step_doc_row[:, :half]) & lower
    docs_second = (step_doc_col[half:] == step_doc_row[:, half:]) & lower
    eye_steps = (iota((steps, steps), 0) == iota((steps, steps), 1)).astype(BF16)

    grams, lefts, work, corners = [], [], [], []
    for local in range(heads_step):
        head = pl.program_id(0) * heads_step + local
        pick = (iota((heads_all, head_depth), 0) == head).astype(BF16)
        lane = slice(local * head_depth, (local + 1) * head_depth)
        query, key, value = query_ref[:, lane], key_ref[:, lane], value_ref[:, lane]
        rate_col = mm(rate_ref[...], pick)
        decay_col = mm(decay_ref[...], pick)
        total_col = mm(step_tri, decay_col)
        token_col = mm(token_tri, decay_col)
        total_row = mm_tn(decay_col, row_tri)[:1]
        rate_row = mm_tn(rate_col, eye_steps)[:1]
        key_one, key_two = key[:half], key[half:]
        gram_one, gram_two = mm_nt(key_one, key_one), mm_nt(key_two, key_two)
        gram_low = mm_nt(key_two, key_one)
        diag_one, diag_two = jnp.where(eye, gram_one, 0.0), jnp.where(eye, gram_two, 0.0)
        inv_row = lax.rsqrt(
            jnp.concatenate(
                [jnp.sum(diag_one, 0, keepdims=True), jnp.sum(diag_two, 0, keepdims=True)], 1
            )
            + 1e-06
        )
        inv_col = lax.rsqrt(
            jnp.concatenate(
                [jnp.sum(diag_one, 1, keepdims=True), jnp.sum(diag_two, 1, keepdims=True)], 0
            )
            + 1e-06
        )
        left = rate_col * inv_col

        def fade(mask, upper, lower_row):
            return jnp.where(mask, jnp.exp(jnp.minimum(upper - lower_row, 0.0)), 0.0)

        part_one = (
            gram_one
            * left[:half]
            * inv_row[:, :half]
            * fade(docs_first, total_col[:half], total_row[:, :half])
        )
        part_two = (
            gram_two
            * left[half:]
            * inv_row[:, half:]
            * fade(docs_second, total_col[half:], total_row[:, half:])
        )
        part_low = (
            gram_low
            * left[half:]
            * inv_row[:, :half]
            * fade(docs_low, total_col[half:], total_row[:, :half])
        )
        grams += [part_one, part_two]
        corners.append(part_low)
        work.append((query, key, value, total_col, token_col, total_row, rate_row, inv_row, inv_col))

    inverses = unit_lower_inverse(grams, half)
    for local in range(heads_step):
        lane = slice(local * head_depth, (local + 1) * head_depth)
        query, key, value, total_col, token_col, total_row, rate_row, inv_row, inv_col = work[local]
        inv_one, inv_two = inverses[2 * local], inverses[2 * local + 1]
        inv_low = -mm(inv_two, mm(corners[local], inv_one))
        start_row = jnp.where(
            step_doc_row == doc_before, jnp.exp(total_row), 0.0
        )
        erase_row = rate_row * start_row * inv_row
        last = total_col[steps - 1 :]
        end_col = jnp.where(step_doc_col == doc_last, jnp.exp(last - total_col), 0.0) * inv_col
        start_token = jnp.where(token_doc_col[:, :half] == doc_before, jnp.exp(token_col), 0.0)

        def solve(scale, right):
            first_rows = mm(inv_one * scale[:, :half], right[:half])
            left = jnp.concatenate([inv_low * scale[:, :half], inv_two * scale[:, half:]], 1)
            return jnp.concatenate([first_rows, mm(left, right)], 0)

        written = solve(rate_row, value)
        erased = solve(erase_row, key)
        token_wide = jnp.concatenate([token_col, token_col], 1)
        scores = mm_nt(query, key) * inv_row * jnp.where(
            score_mask, jnp.exp(jnp.minimum(token_wide - total_row, 0.0)), 0.0
        )
        scores = scores.astype(BF16)
        inner_ref[:, lane] = mm(scores, written)
        carried_ref[:, lane] = (
            start_token * query.astype(F32) - mm(scores, erased)
        ).astype(carried_ref.dtype)
        last_gain = jnp.where(doc_last == doc_before, jnp.exp(last), 0.0)
        state_ref[local, 0] = (jnp.where(eye, last_gain, 0.0) - mm_tn(key, erased * end_col)).astype(
            state_ref.dtype
        )
        state_ref[local, 1] = mm_tn(key, written * end_col).astype(state_ref.dtype)


def local_pieces(queries, keys, values, write_rate, log_decay, doc_starts):
    tokens, width = queries.shape
    heads_all = log_decay.shape[1]
    head_depth = width // heads_all
    heads_step = 2
    lanes = heads_step * head_depth
    steps = 2 * tokens
    return pl.pallas_call(
        functools.partial(piece_kernel, heads_step=heads_step, head_depth=head_depth),
        grid=(heads_all // heads_step,),
        in_specs=[
            pl.BlockSpec(memory_space=pltpu.SMEM),
            pl.BlockSpec((tokens, lanes), lambda i: (0, i)),
            pl.BlockSpec((steps, lanes), lambda i: (0, i)),
            pl.BlockSpec((steps, lanes), lambda i: (0, i)),
            pl.BlockSpec((steps, heads_all), lambda i: (0, 0)),
            pl.BlockSpec((tokens, heads_all), lambda i: (0, 0)),
        ],
        out_specs=[
            pl.BlockSpec((tokens, lanes), lambda i: (0, i)),
            pl.BlockSpec((tokens, lanes), lambda i: (0, i)),
            pl.BlockSpec((heads_step, 2, head_depth, head_depth), lambda i: (i, 0, 0, 0)),
        ],
        out_shape=[
            jax.ShapeDtypeStruct((tokens, width), F32),
            jax.ShapeDtypeStruct((tokens, width), BF16),
            jax.ShapeDtypeStruct((heads_all, 2, head_depth, head_depth), BF16),
        ],
        compiler_params=pltpu.CompilerParams(vmem_limit_bytes=40 * 1024 * 1024),
        name="pieces",
    )(
        doc_starts,
        queries,
        keys.reshape(steps, width),
        values.reshape(steps, width),
        write_rate.reshape(steps, heads_all),
        log_decay,
    )


def passed_along(value, axis, steps):
    count = lax.axis_size(axis)
    return lax.ppermute(value, axis, [(source, source + steps) for source in range(count - steps)])


def on_device(
    queries, keys, values, out_gate, write_rate, log_decay, doc_starts, norm_gain, out_weight
):
    tokens, width = queries.shape
    heads_all = log_decay.shape[1]
    head_depth = width // heads_all
    groups = lax.axis_size("head")
    inner, carried, states = local_pieces(
        queries, keys, values, write_rate, log_decay, doc_starts
    )
    mine = lax.all_to_all(states, "head", split_axis=0, concat_axis=0, tiled=True)
    mine = mine.reshape(groups, heads_all // groups, 2, head_depth, head_depth)

    def step(maps, state, index):
        return jnp.einsum(
            "hde,hef->hdf", maps, state.astype(BF16), preferred_element_type=F32
        ) + mine[index, :, 1].astype(F32)

    def sweep(incoming):
        states_in = [incoming]
        for index in range(groups):
            states_in.append(step(mine[index, :, 0], states_in[-1], index))
        return states_in

    incoming = jnp.zeros(mine.shape[1:2] + mine.shape[3:], F32)
    for _ in range(lax.axis_size("seq") // 2):
        incoming = passed_along(sweep(incoming)[-1].astype(BF16), "seq", 1).astype(F32)
    starts = jnp.stack(sweep(incoming)[:groups]).astype(BF16)
    starts = starts.reshape(heads_all, head_depth, head_depth)
    back = lax.all_to_all(starts, "head", split_axis=0, concat_axis=0, tiled=True)
    readout = inner.reshape(tokens, heads_all, head_depth) + jnp.einsum(
        "thd,hde->the",
        carried.reshape(tokens, heads_all, head_depth),
        back,
        preferred_element_type=F32,
    )
    gate_vals = out_gate.reshape(tokens, heads_all, head_depth).astype(F32)
    inv_rms = lax.rsqrt(jnp.mean(readout * readout, -1, keepdims=True) + 1e-05)
    normed = (readout * inv_rms * norm_gain * jax.nn.silu(gate_vals)).astype(BF16)
    normed = normed.reshape(tokens, width)
    acc_total = jnp.dot(
        lax.all_gather(normed, "head", axis=0, tiled=True), out_weight, preferred_element_type=F32
    )
    return acc_total.astype(BF16)


def solution(mesh):
    placed = (
        P(("rep", "seq", "head"), None),
        P(("rep", "seq", "head"), None, None),
        P(("rep", "seq", "head"), None, None),
        P(("rep", "seq", "head"), None),
        P(("rep", "seq", "head"), None, None),
        P(("rep", "seq", "head"), None),
        P("rep"),
        P(),
        P(None, "head"),
    )
    return jax.shard_map(
        on_device, mesh=mesh, in_specs=placed, out_specs=P(("rep", "seq"), "head"), check_vma=False
    )
```

```python
import functools

import jax
import jax.numpy as jnp
from jax import lax
from jax.experimental import pallas as pl
from jax.experimental.pallas import tpu as pltpu
from jax.sharding import PartitionSpec as P

F32 = jnp.float32
BF16 = jnp.bfloat16


def mm(a, b):
    return jnp.dot(a.astype(BF16), b.astype(BF16), preferred_element_type=F32)


def mm_nt(a, b):
    return lax.dot_general(
        a.astype(BF16), b.astype(BF16), (((1,), (1,)), ((), ())), preferred_element_type=F32
    )


def mm_tn(a, b):
    return lax.dot_general(
        a.astype(BF16), b.astype(BF16), (((0,), (0,)), ((), ())), preferred_element_type=F32
    )


def iota(shape, dim):
    return lax.broadcasted_iota(jnp.int32, shape, dim)


def unit_lower_inverse(parts, half):
    rows, cols = iota((half, half), 0), iota((half, half), 1)
    size = 1
    inverses = None
    while size < half:
        row_block, col_block = rows // size, cols // size
        link = (row_block == col_block + 1) & (row_block % 2 == 1)
        linked = [jnp.where(link, part, 0.0) for part in parts]
        if inverses is None:
            eye = jnp.where(rows == cols, 1.0, 0.0)
            inverses = [eye - part for part in linked]
        else:
            short = [inverse.astype(BF16) for inverse in inverses]
            middle = [mm(part, inverse) for part, inverse in zip(linked, short)]
            fixes = [mm(inverse, part) for inverse, part in zip(short, middle)]
            inverses = [inverse - fix for inverse, fix in zip(inverses, fixes)]
        size *= 2
    return inverses


def piece_kernel(
    doc_ref,
    query_ref,
    key_ref,
    value_ref,
    rate_ref,
    decay_ref,
    inner_ref,
    carried_ref,
    state_ref,
    *,
    heads_step,
    head_depth,
):
    tokens = query_ref.shape[0]
    steps = 2 * tokens
    half = steps // 2
    heads_all = rate_ref.shape[1]
    docs = doc_ref.shape[0]
    first = (lax.axis_index("seq") * lax.axis_size("head") + lax.axis_index("head")) * tokens

    def doc_of(position):
        return sum((position >= doc_ref[index]).astype(jnp.int32) for index in range(docs))

    doc_before = doc_of(first - 1)
    doc_last = doc_of(first + tokens - 1)
    step_doc_col = doc_of(first + iota((steps, half), 0) // 2)
    step_doc_row = doc_of(first + iota((1, steps), 1) // 2)
    token_doc_col = doc_of(first + iota((tokens, steps), 0))
    col_ids = iota((tokens, steps), 1)
    score_mask = (col_ids <= 2 * iota((tokens, steps), 0) + 1) & (token_doc_col == step_doc_row)
    step_tri = (iota((steps, tokens), 1) <= iota((steps, tokens), 0) // 2).astype(BF16)
    token_tri = (iota((tokens, tokens), 1) <= iota((tokens, tokens), 0)).astype(BF16)
    row_tri = (iota((tokens, steps), 0) <= iota((tokens, steps), 1) // 2).astype(BF16)
    rows, cols = iota((half, half), 0), iota((half, half), 1)
    eye = rows == cols
    lower = rows > cols
    docs_low = step_doc_col[half:] == step_doc_row[:, :half]
    docs_first = (step_doc_col[:half] == step_doc_row[:, :half]) & lower
    docs_second = (step_doc_col[half:] == step_doc_row[:, half:]) & lower
    eye_steps = (iota((steps, steps), 0) == iota((steps, steps), 1)).astype(BF16)

    grams, lefts, work, corners = [], [], [], []
    for local in range(heads_step):
        head = pl.program_id(0) * heads_step + local
        pick = (iota((heads_all, head_depth), 0) == head).astype(BF16)
        lane = slice(local * head_depth, (local + 1) * head_depth)
        query, key, value = query_ref[:, lane], key_ref[:, lane], value_ref[:, lane]
        rate_col = mm(rate_ref[...], pick)
        decay_col = mm(decay_ref[...], pick)
        total_col = mm(step_tri, decay_col)
        token_col = mm(token_tri, decay_col)
        total_row = mm_tn(decay_col, row_tri)[:1]
        rate_row = mm_tn(rate_col, eye_steps)[:1]
        key_one, key_two = key[:half], key[half:]
        gram_one, gram_two = mm_nt(key_one, key_one), mm_nt(key_two, key_two)
        gram_low = mm_nt(key_two, key_one)
        diag_one, diag_two = jnp.where(eye, gram_one, 0.0), jnp.where(eye, gram_two, 0.0)
        inv_row = lax.rsqrt(
            jnp.concatenate(
                [jnp.sum(diag_one, 0, keepdims=True), jnp.sum(diag_two, 0, keepdims=True)], 1
            )
            + 1e-06
        )
        inv_col = lax.rsqrt(
            jnp.concatenate(
                [jnp.sum(diag_one, 1, keepdims=True), jnp.sum(diag_two, 1, keepdims=True)], 0
            )
            + 1e-06
        )
        left = rate_col * inv_col

        def fade(mask, upper, lower_row):
            return jnp.where(mask, jnp.exp(jnp.minimum(upper - lower_row, 0.0)), 0.0)

        part_one = (
            gram_one
            * left[:half]
            * inv_row[:, :half]
            * fade(docs_first, total_col[:half], total_row[:, :half])
        )
        part_two = (
            gram_two
            * left[half:]
            * inv_row[:, half:]
            * fade(docs_second, total_col[half:], total_row[:, half:])
        )
        part_low = (
            gram_low
            * left[half:]
            * inv_row[:, :half]
            * fade(docs_low, total_col[half:], total_row[:, :half])
        )
        grams += [part_one, part_two]
        corners.append(part_low)
        work.append((query, key, value, total_col, token_col, total_row, rate_row, inv_row, inv_col))

    inverses = unit_lower_inverse(grams, half)
    for local in range(heads_step):
        lane = slice(local * head_depth, (local + 1) * head_depth)
        query, key, value, total_col, token_col, total_row, rate_row, inv_row, inv_col = work[local]
        inv_one, inv_two = inverses[2 * local], inverses[2 * local + 1]
        inv_low = -mm(inv_two, mm(corners[local], inv_one))
        start_row = jnp.where(
            step_doc_row == doc_before, jnp.exp(total_row), 0.0
        )
        erase_row = rate_row * start_row * inv_row
        last = total_col[steps - 1 :]
        end_col = jnp.where(step_doc_col == doc_last, jnp.exp(last - total_col), 0.0) * inv_col
        start_token = jnp.where(token_doc_col[:, :half] == doc_before, jnp.exp(token_col), 0.0)

        def solve(scale, right):
            first_rows = mm(inv_one * scale[:, :half], right[:half])
            left = jnp.concatenate([inv_low * scale[:, :half], inv_two * scale[:, half:]], 1)
            return jnp.concatenate([first_rows, mm(left, right)], 0)

        written = solve(rate_row, value)
        erased = solve(erase_row, key)
        token_wide = jnp.concatenate([token_col, token_col], 1)
        scores = mm_nt(query, key) * inv_row * jnp.where(
            score_mask, jnp.exp(jnp.minimum(token_wide - total_row, 0.0)), 0.0
        )
        scores = scores.astype(BF16)
        inner_ref[:, lane] = mm(scores, written)
        carried_ref[:, lane] = (
            start_token * query.astype(F32) - mm(scores, erased)
        ).astype(carried_ref.dtype)
        last_gain = jnp.where(doc_last == doc_before, jnp.exp(last), 0.0)
        state_ref[local, 0] = (jnp.where(eye, last_gain, 0.0) - mm_tn(key, erased * end_col)).astype(
            state_ref.dtype
        )
        state_ref[local, 1] = mm_tn(key, written * end_col).astype(state_ref.dtype)


def local_pieces(queries, keys, values, write_rate, log_decay, doc_starts):
    tokens, width = queries.shape
    heads_all = log_decay.shape[1]
    head_depth = width // heads_all
    heads_step = 2
    lanes = heads_step * head_depth
    steps = 2 * tokens
    return pl.pallas_call(
        functools.partial(piece_kernel, heads_step=heads_step, head_depth=head_depth),
        grid=(heads_all // heads_step,),
        in_specs=[
            pl.BlockSpec(memory_space=pltpu.SMEM),
            pl.BlockSpec((tokens, lanes), lambda i: (0, i)),
            pl.BlockSpec((steps, lanes), lambda i: (0, i)),
            pl.BlockSpec((steps, lanes), lambda i: (0, i)),
            pl.BlockSpec((steps, heads_all), lambda i: (0, 0)),
            pl.BlockSpec((tokens, heads_all), lambda i: (0, 0)),
        ],
        out_specs=[
            pl.BlockSpec((tokens, lanes), lambda i: (0, i)),
            pl.BlockSpec((tokens, lanes), lambda i: (0, i)),
            pl.BlockSpec((heads_step, 2, head_depth, head_depth), lambda i: (i, 0, 0, 0)),
        ],
        out_shape=[
            jax.ShapeDtypeStruct((tokens, width), F32),
            jax.ShapeDtypeStruct((tokens, width), BF16),
            jax.ShapeDtypeStruct((heads_all, 2, head_depth, head_depth), BF16),
        ],
        compiler_params=pltpu.CompilerParams(vmem_limit_bytes=40 * 1024 * 1024),
        name="pieces",
    )(
        doc_starts,
        queries,
        keys.reshape(steps, width),
        values.reshape(steps, width),
        write_rate.reshape(steps, heads_all),
        log_decay,
    )


MESH = pl.DeviceIdType.MESH


def join_kernel(
    inner_ref,
    carried_ref,
    state_ref,
    gate_ref,
    gain_ref,
    weight_ref,
    out_ref,
    mine,
    relay_out,
    relay_in,
    starts,
    back,
    normed,
    deal_send,
    deal_recv,
    relay_send,
    relay_recv,
    back_send,
    back_recv,
    far_send,
    far_recv,
    near_send,
    near_recv,
):
    groups, heads_here, _, depth, _ = mine.shape
    hops = relay_in.shape[0]
    tokens = inner_ref.shape[0]
    block = heads_here * depth
    me, place, places = lax.axis_index("head"), lax.axis_index("seq"), lax.axis_size("seq")
    has_next, has_prior = place < places - 1, place > 0
    chips = groups // 2
    sibling = me + 1 - 2 * lax.rem(me, 2)

    def to_head(source, target, send, recv, peer):
        return pltpu.make_async_remote_copy(
            src_ref=source,
            dst_ref=target,
            send_sem=send,
            recv_sem=recv,
            device_id={"head": peer},
            device_id_type=MESH,
        )

    barrier = pltpu.get_barrier_semaphore()
    for offset in range(1, groups):
        pl.semaphore_signal(
            barrier, inc=1, device_id={"head": lax.rem(me + offset, groups)}, device_id_type=MESH
        )

    @pl.when(has_next)
    def _():
        pl.semaphore_signal(barrier, inc=1, device_id={"seq": place + 1}, device_id_type=MESH)

    @pl.when(has_prior)
    def _():
        pl.semaphore_signal(barrier, inc=1, device_id={"seq": place - 1}, device_id_type=MESH)

    pl.semaphore_wait(
        barrier, groups - 1 + has_next.astype(jnp.int32) + has_prior.astype(jnp.int32)
    )

    deals = []
    for offset in range(1, groups):
        peer = lax.rem(me + offset, groups)
        copy = to_head(
            state_ref.at[pl.ds(peer * heads_here, heads_here)],
            mine.at[me],
            deal_send.at[offset],
            deal_recv.at[offset],
            peer,
        )
        copy.start()
        deals.append(copy)
    mine[me] = state_ref[pl.ds(me * heads_here, heads_here)]

    @pl.when(place == 0)
    def _():
        relay_in[...] = jnp.zeros_like(relay_in)

    for copy in deals:
        copy.wait_recv()

    sums, maps = [], []
    for local in range(heads_here):
        chain = [None, mine[0, local, 1].astype(F32)]
        for index in range(1, groups):
            chain.append(
                mm(mine[index, local, 0], chain[-1]) + mine[index, local, 1].astype(F32)
            )
        sums.append(chain)

    def relay(hop):
        return pltpu.make_async_remote_copy(
            src_ref=relay_out.at[hop],
            dst_ref=relay_in.at[hop],
            send_sem=relay_send.at[hop],
            recv_sem=relay_recv.at[hop],
            device_id={"seq": place + 1},
            device_id_type=MESH,
        )

    for hop in range(hops):
        for local in range(heads_here):
            value = sums[local][groups]
            if hop:
                value = value + mm(maps[local][groups], relay_in[hop - 1, local])
            relay_out[hop, local] = value.astype(BF16)

        @pl.when(has_next)
        def _(hop=hop):
            relay(hop).start()

        if hop == 0:
            for local in range(heads_here):
                chain = [None, mine[0, local, 0]]
                for index in range(1, groups):
                    chain.append(mm(mine[index, local, 0], chain[-1]).astype(BF16))
                maps.append(chain)

        @pl.when(has_prior)
        def _(hop=hop):
            relay(hop).wait_recv()

    for local in range(heads_here):
        incoming = relay_in[hops - 1, local]
        starts[0, local] = incoming
        for index in range(1, groups):
            starts[index, local] = (
                mm(maps[local][index], incoming) + sums[local][index]
            ).astype(BF16)
    returns = []
    for offset in range(1, groups):
        peer = lax.rem(me + offset, groups)
        copy = to_head(
            starts.at[peer], back.at[me], back_send.at[offset], back_recv.at[offset], peer
        )
        copy.start()
        returns.append(copy)
    back[me] = starts[me]

    gain = gain_ref[...]
    fars, nears = [], []
    for piece in range(groups):
        if piece:
            returns[piece - 1].wait_recv()
        owner = lax.rem(me - piece + groups, groups)
        for local in range(heads_here):
            lanes = pl.ds(pl.multiple_of(owner * block + local * depth, depth), depth)
            readout = inner_ref[:, lanes] + mm(carried_ref[:, lanes], back[owner, local])
            gate = gate_ref[:, lanes].astype(F32)
            inv_rms = lax.rsqrt(jnp.mean(readout * readout, -1, keepdims=True) + 1e-05)
            normed[me, :, lanes] = (
                readout * inv_rms * gain * (gate / (1.0 + jnp.exp(-gate)))
            ).astype(BF16)
        lanes = pl.ds(pl.multiple_of(owner * block, block), block)
        here = normed.at[me, :, lanes]
        for chip in range(1, chips):
            copy = to_head(
                here,
                here,
                far_send.at[piece, chip],
                far_recv.at[piece, chip],
                lax.rem(me + 2 * chip, groups),
            )
            copy.start()
            fars.append((chip, piece, copy))
        copy = to_head(here, here, near_send.at[piece, 0], near_recv.at[piece, 0], sibling)
        copy.start()
        nears.append(copy)

    def project(source):
        rows = pl.ds(pl.multiple_of(source * tokens, tokens), tokens)
        out_ref[rows, :] = jnp.dot(
            normed[source], weight_ref[...], preferred_element_type=F32
        ).astype(out_ref.dtype)

    project(me)
    forwards = []
    for chip, piece, copy in fars:
        source = lax.rem(me - 2 * chip + groups, groups)
        owner = lax.rem(source - piece + groups, groups)
        there = normed.at[source, :, pl.ds(pl.multiple_of(owner * block, block), block)]
        copy.wait_recv()
        onward = to_head(
            there, there, near_send.at[piece, chip], near_recv.at[piece, chip], sibling
        )
        onward.start()
        forwards.append(onward)
    for copy in nears:
        copy.wait_recv()
    project(sibling)
    for chip in range(1, chips):
        project(lax.rem(me - 2 * chip + groups, groups))
    for onward in forwards:
        onward.wait_recv()
    for chip in range(1, chips):
        project(lax.rem(sibling - 2 * chip + groups, groups))

    for copy in deals + returns + [far[2] for far in fars] + nears + forwards:
        copy.wait_send()
    for hop in range(hops):

        @pl.when(has_next)
        def _(hop=hop):
            relay(hop).wait_send()


def on_device(
    queries, keys, values, out_gate, write_rate, log_decay, doc_starts, norm_gain, out_weight
):
    tokens, width = queries.shape
    heads_all = log_decay.shape[1]
    depth = width // heads_all
    groups = lax.axis_size("head")
    heads_here = heads_all // groups
    hops = lax.axis_size("seq") // 2
    inner, carried, states = local_pieces(
        queries, keys, values, write_rate, log_decay, doc_starts
    )
    sems = pltpu.SemaphoreType.DMA
    return pl.pallas_call(
        join_kernel,
        in_specs=[pl.BlockSpec(memory_space=pltpu.VMEM)] * 6,
        out_specs=pl.BlockSpec(memory_space=pltpu.VMEM),
        out_shape=jax.ShapeDtypeStruct((groups * tokens, out_weight.shape[1]), BF16),
        scratch_shapes=[
            pltpu.VMEM((groups, heads_here, 2, depth, depth), BF16),
            pltpu.VMEM((hops, heads_here, depth, depth), BF16),
            pltpu.VMEM((hops, heads_here, depth, depth), BF16),
            pltpu.VMEM((groups, heads_here, depth, depth), BF16),
            pltpu.VMEM((groups, heads_here, depth, depth), BF16),
            pltpu.VMEM((groups, tokens, width), BF16),
            sems((groups,)),
            sems((groups,)),
            sems((hops,)),
            sems((hops,)),
            sems((groups,)),
            sems((groups,)),
            sems((groups, groups // 2)),
            sems((groups, groups // 2)),
            sems((groups, groups // 2)),
            sems((groups, groups // 2)),
        ],
        compiler_params=pltpu.CompilerParams(
            collective_id=0, has_side_effects=True, vmem_limit_bytes=40 * 1024 * 1024
        ),
        name="join",
    )(inner, carried, states, out_gate, norm_gain.reshape(1, depth), out_weight)


def solution(mesh):
    placed = (
        P(("rep", "seq", "head"), None),
        P(("rep", "seq", "head"), None, None),
        P(("rep", "seq", "head"), None, None),
        P(("rep", "seq", "head"), None),
        P(("rep", "seq", "head"), None, None),
        P(("rep", "seq", "head"), None),
        P("rep"),
        P(),
        P(None, "head"),
    )
    return jax.shard_map(
        on_device, mesh=mesh, in_specs=placed, out_specs=P(("rep", "seq"), "head"), check_vma=False
    )
```

```python
import jax
import jax.numpy as jnp
from jax import lax
from jax.experimental import pallas as pl
from jax.experimental.pallas import tpu as pltpu
from jax.sharding import PartitionSpec as P

F32 = jnp.float32
BF16 = jnp.bfloat16


def mm(a, b):
    return jnp.dot(a.astype(BF16), b.astype(BF16), preferred_element_type=F32)


def mm_nt(a, b):
    return lax.dot_general(
        a.astype(BF16), b.astype(BF16), (((1,), (1,)), ((), ())), preferred_element_type=F32
    )


def mm_tn(a, b):
    return lax.dot_general(
        a.astype(BF16), b.astype(BF16), (((0,), (0,)), ((), ())), preferred_element_type=F32
    )


def iota(shape, dim):
    return lax.broadcasted_iota(jnp.int32, shape, dim)


def unit_lower_inverse(parts, half):
    rows, cols = iota((half, half), 0), iota((half, half), 1)
    size = 1
    inverses = None
    while size < half:
        row_block, col_block = rows // size, cols // size
        link = (row_block == col_block + 1) & (row_block % 2 == 1)
        linked = [jnp.where(link, part, 0.0) for part in parts]
        if inverses is None:
            eye = jnp.where(rows == cols, 1.0, 0.0)
            inverses = [eye - part for part in linked]
        else:
            short = [inverse.astype(BF16) for inverse in inverses]
            middle = [mm(part, inverse) for part, inverse in zip(linked, short)]
            fixes = [mm(inverse, part) for inverse, part in zip(short, middle)]
            inverses = [inverse - fix for inverse, fix in zip(inverses, fixes)]
        size *= 2
    return inverses


class Frame:
    def __init__(self, doc_ref, tokens, first):
        steps, half = 2 * tokens, tokens
        docs = doc_ref.shape[0]

        def doc_of(position):
            return sum((position >= doc_ref[index]).astype(jnp.int32) for index in range(docs))

        self.tokens, self.steps, self.half = tokens, steps, half
        self.doc_before = doc_of(first - 1)
        self.doc_last = doc_of(first + tokens - 1)
        self.step_doc_col = doc_of(first + iota((steps, half), 0) // 2)
        self.step_doc_row = doc_of(first + iota((1, steps), 1) // 2)
        self.token_doc_col = doc_of(first + iota((tokens, steps), 0))
        col_ids = iota((tokens, steps), 1)
        self.score_mask = (col_ids <= 2 * iota((tokens, steps), 0) + 1) & (
            self.token_doc_col == self.step_doc_row
        )
        self.step_tri = (iota((steps, tokens), 1) <= iota((steps, tokens), 0) // 2).astype(BF16)
        self.token_tri = (iota((tokens, tokens), 1) <= iota((tokens, tokens), 0)).astype(BF16)
        self.row_tri = (iota((tokens, steps), 0) <= iota((tokens, steps), 1) // 2).astype(BF16)
        rows, cols = iota((half, half), 0), iota((half, half), 1)
        self.eye = rows == cols
        lower = rows > cols
        self.docs_low = self.step_doc_col[half:] == self.step_doc_row[:, :half]
        self.docs_first = (self.step_doc_col[:half] == self.step_doc_row[:, :half]) & lower
        self.docs_second = (self.step_doc_col[half:] == self.step_doc_row[:, half:]) & lower
        self.eye_steps = (iota((steps, steps), 0) == iota((steps, steps), 1)).astype(BF16)


def head_lanes(head, depth):
    return pl.ds(pl.multiple_of(head * depth, depth), depth)


def head_decay(frame, decay_ref, head, depth):
    pick = (iota((decay_ref.shape[1], depth), 0) == head).astype(BF16)
    decay_col = mm(decay_ref[...], pick)
    return decay_col, mm_tn(decay_col, frame.row_tri)[:1]


def state_phase(frame, heads, key_ref, value_ref, rate_ref, decay_ref, keep, state_ref, depth):
    half, steps = frame.half, frame.steps
    parts, corners, work = [], [], []
    for head in heads:
        pick = (iota((rate_ref.shape[1], depth), 0) == head).astype(BF16)
        lanes = head_lanes(head, depth)
        key, value = key_ref[:, lanes], value_ref[:, lanes]
        rate_col = mm(rate_ref[...], pick)
        decay_col, total_row = head_decay(frame, decay_ref, head, depth)
        total_col = mm(frame.step_tri, decay_col)
        rate_row = mm_tn(rate_col, frame.eye_steps)[:1]
        key_one, key_two = key[:half], key[half:]
        gram_one, gram_two = mm_nt(key_one, key_one), mm_nt(key_two, key_two)
        gram_low = mm_nt(key_two, key_one)
        diag_one = jnp.where(frame.eye, gram_one, 0.0)
        diag_two = jnp.where(frame.eye, gram_two, 0.0)
        inv_row = lax.rsqrt(
            jnp.concatenate(
                [jnp.sum(diag_one, 0, keepdims=True), jnp.sum(diag_two, 0, keepdims=True)], 1
            )
            + 1e-06
        )
        inv_col = lax.rsqrt(
            jnp.concatenate(
                [jnp.sum(diag_one, 1, keepdims=True), jnp.sum(diag_two, 1, keepdims=True)], 0
            )
            + 1e-06
        )
        left = rate_col * inv_col

        def linked(gram, mask, rows, cols):
            ratio = jnp.exp(jnp.minimum(total_col[rows] - total_row[:, cols], 0.0))
            return jnp.where(mask, gram * left[rows] * inv_row[:, cols] * ratio, 0.0)

        upper, lower = slice(0, half), slice(half, steps)
        parts.append(linked(gram_one, frame.docs_first, upper, upper))
        parts.append(linked(gram_two, frame.docs_second, lower, lower))
        corners.append(linked(gram_low, frame.docs_low, lower, upper))
        work.append((key, value, total_col, total_row, rate_row, inv_row, inv_col))

    inverses = unit_lower_inverse(parts, half)
    for local, head in enumerate(heads):
        key, value, total_col, total_row, rate_row, inv_row, inv_col = work[local]
        inv_one, inv_two = inverses[2 * local], inverses[2 * local + 1]
        inv_low = -mm(inv_two, mm(corners[local], inv_one))
        start_row = jnp.where(
            frame.step_doc_row == frame.doc_before, jnp.exp(total_row), 0.0
        )
        last = total_col[steps - 1 :]
        end_col = inv_col * jnp.where(
            frame.step_doc_col == frame.doc_last, jnp.exp(last - total_col), 0.0
        )

        def solve(scale, right):
            first_rows = mm(inv_one * scale[:, :half], right[:half])
            left = jnp.concatenate([inv_low * scale[:, :half], inv_two * scale[:, half:]], 1)
            return jnp.concatenate([first_rows, mm(left, right)], 0)

        written = solve(rate_row, value)
        erased = solve(rate_row * start_row * inv_row, key)
        last_gain = jnp.where(frame.doc_last == frame.doc_before, jnp.exp(last), 0.0)
        state_ref[head, 0] = (
            jnp.where(frame.eye, last_gain, 0.0) - mm_tn(key, erased * end_col)
        ).astype(BF16)
        state_ref[head, 1] = mm_tn(key, written * end_col).astype(BF16)
        written_ref, erased_ref, inverse_ref = keep
        written_ref[head] = written.astype(BF16)
        erased_ref[head] = erased.astype(BF16)
        inverse_ref[head] = inv_row


def read_phase(frame, head, query_ref, key_ref, decay_ref, keep, inner_ref, carried_ref, depth):
    written_ref, erased_ref, inverse_ref = keep
    lanes = head_lanes(head, depth)
    query, key = query_ref[:, lanes], key_ref[:, lanes]
    decay_col, total_row = head_decay(frame, decay_ref, head, depth)
    token_col = mm(frame.token_tri, decay_col)
    token_wide = jnp.concatenate([token_col, token_col], 1)
    start_token = jnp.where(
        frame.token_doc_col[:, : frame.half] == frame.doc_before, jnp.exp(token_col), 0.0
    )
    ratio = jnp.exp(jnp.minimum(token_wide - total_row, 0.0))
    scores = jnp.where(frame.score_mask, mm_nt(query, key) * inverse_ref[head] * ratio, 0.0)
    scores = scores.astype(BF16)
    inner_ref[:, lanes] = mm(scores, written_ref[head])
    carried_ref[:, lanes] = (
        start_token * query.astype(F32) - mm(scores, erased_ref[head])
    ).astype(carried_ref.dtype)


MESH = pl.DeviceIdType.MESH


def join_kernel(
    doc_ref,
    query_ref,
    key_ref,
    value_ref,
    rate_ref,
    decay_ref,
    gate_ref,
    gain_ref,
    weight_ref,
    out_ref,
    inner_ref,
    carried_ref,
    state_ref,
    written_ref,
    erased_ref,
    inverse_ref,
    mine,
    relay_out,
    relay_in,
    starts,
    back,
    normed,
    deal_send,
    deal_recv,
    relay_send,
    relay_recv,
    back_send,
    back_recv,
    far_send,
    far_recv,
    near_send,
    near_recv,
):
    groups, heads_here, _, depth, _ = mine.shape
    hops = relay_in.shape[0]
    heads_all = groups * heads_here
    tokens = query_ref.shape[0]
    block = heads_here * depth
    me, place, places = lax.axis_index("head"), lax.axis_index("seq"), lax.axis_size("seq")
    has_next, has_prior = place < places - 1, place > 0
    chips = groups // 2
    sibling = me + 1 - 2 * lax.rem(me, 2)

    def to_head(source, target, send, recv, peer):
        return pltpu.make_async_remote_copy(
            src_ref=source,
            dst_ref=target,
            send_sem=send,
            recv_sem=recv,
            device_id={"head": peer},
            device_id_type=MESH,
        )

    barrier = pltpu.get_barrier_semaphore()
    for offset in range(1, groups):
        pl.semaphore_signal(
            barrier, inc=1, device_id={"head": lax.rem(me + offset, groups)}, device_id_type=MESH
        )

    @pl.when(has_next)
    def _():
        pl.semaphore_signal(barrier, inc=1, device_id={"seq": place + 1}, device_id_type=MESH)

    @pl.when(has_prior)
    def _():
        pl.semaphore_signal(barrier, inc=1, device_id={"seq": place - 1}, device_id_type=MESH)

    @pl.when(place == 0)
    def _():
        relay_in[...] = jnp.zeros_like(relay_in)

    frame = Frame(doc_ref, tokens, (place * groups + me) * tokens)
    keep = (written_ref, erased_ref, inverse_ref)
    order = []
    for chip in range(1, chips):
        order += [lax.rem(me + 2 * chip, groups), lax.rem(sibling + 2 * chip, groups)]
    order += [sibling, me]
    together = max(1, 4 // heads_here)
    deals = []
    for begin in range(0, groups, together):
        batch = list(range(begin, min(begin + together, groups)))
        heads = [order[spot] * heads_here + local for spot in batch for local in range(heads_here)]
        state_phase(
            frame, heads, key_ref, value_ref, rate_ref, decay_ref, keep, state_ref, depth
        )
        if begin == 0:
            pl.semaphore_wait(
                barrier, groups - 1 + has_next.astype(jnp.int32) + has_prior.astype(jnp.int32)
            )
        for spot in batch:
            if spot == groups - 1:
                continue
            copy = to_head(
                state_ref.at[pl.ds(order[spot] * heads_here, heads_here)],
                mine.at[me],
                deal_send.at[spot],
                deal_recv.at[spot],
                order[spot],
            )
            copy.start()
            deals.append(copy)
    mine[me] = state_ref[pl.ds(me * heads_here, heads_here)]

    for copy in deals:
        copy.wait_recv()

    sums, maps = [], []
    for local in range(heads_here):
        chain = [None, mine[0, local, 1].astype(F32)]
        for index in range(1, groups):
            chain.append(
                mm(mine[index, local, 0], chain[-1]) + mine[index, local, 1].astype(F32)
            )
        sums.append(chain)

    def relay(hop):
        return pltpu.make_async_remote_copy(
            src_ref=relay_out.at[hop],
            dst_ref=relay_in.at[hop],
            send_sem=relay_send.at[hop],
            recv_sem=relay_recv.at[hop],
            device_id={"seq": place + 1},
            device_id_type=MESH,
        )

    for hop in range(hops):
        for local in range(heads_here):
            value = sums[local][groups]
            if hop:
                value = value + mm(maps[local][groups], relay_in[hop - 1, local])
            relay_out[hop, local] = value.astype(BF16)

        @pl.when(has_next)
        def _(hop=hop):
            relay(hop).start()

        if hop == 0:
            for local in range(heads_here):
                chain = [None, mine[0, local, 0]]
                for index in range(1, groups):
                    chain.append(mm(mine[index, local, 0], chain[-1]).astype(BF16))
                maps.append(chain)

        for head in range(heads_all * hop // hops, heads_all * (hop + 1) // hops):
            read_phase(
                frame, head, query_ref, key_ref, decay_ref, keep, inner_ref, carried_ref, depth
            )

        @pl.when(has_prior)
        def _(hop=hop):
            relay(hop).wait_recv()

    for local in range(heads_here):
        incoming = relay_in[hops - 1, local]
        starts[0, local] = incoming
        for index in range(1, groups):
            starts[index, local] = (
                mm(maps[local][index], incoming) + sums[local][index]
            ).astype(BF16)
    returns = []
    for offset in range(1, groups):
        peer = lax.rem(me + offset, groups)
        copy = to_head(
            starts.at[peer], back.at[me], back_send.at[offset], back_recv.at[offset], peer
        )
        copy.start()
        returns.append(copy)
    back[me] = starts[me]

    gain = gain_ref[...]
    fars, nears = [], []
    for piece in range(groups):
        if piece:
            returns[piece - 1].wait_recv()
        owner = lax.rem(me - piece + groups, groups)
        for local in range(heads_here):
            lanes = pl.ds(pl.multiple_of(owner * block + local * depth, depth), depth)
            readout = inner_ref[:, lanes] + mm(carried_ref[:, lanes], back[owner, local])
            gate = gate_ref[:, lanes].astype(F32)
            inv_rms = lax.rsqrt(jnp.mean(readout * readout, -1, keepdims=True) + 1e-05)
            normed[me, :, lanes] = (
                readout * inv_rms * gain * (gate / (1.0 + jnp.exp(-gate)))
            ).astype(BF16)
        lanes = pl.ds(pl.multiple_of(owner * block, block), block)
        here = normed.at[me, :, lanes]
        for chip in range(1, chips):
            copy = to_head(
                here,
                here,
                far_send.at[piece, chip],
                far_recv.at[piece, chip],
                lax.rem(me + 2 * chip, groups),
            )
            copy.start()
            fars.append((chip, piece, copy))
        copy = to_head(here, here, near_send.at[piece, 0], near_recv.at[piece, 0], sibling)
        copy.start()
        nears.append(copy)

    def project(source):
        rows = pl.ds(pl.multiple_of(source * tokens, tokens), tokens)
        out_ref[rows, :] = jnp.dot(
            normed[source], weight_ref[...], preferred_element_type=F32
        ).astype(out_ref.dtype)

    project(me)
    forwards = []
    for chip, piece, copy in fars:
        source = lax.rem(me - 2 * chip + groups, groups)
        owner = lax.rem(source - piece + groups, groups)
        there = normed.at[source, :, pl.ds(pl.multiple_of(owner * block, block), block)]
        copy.wait_recv()
        onward = to_head(
            there, there, near_send.at[piece, chip], near_recv.at[piece, chip], sibling
        )
        onward.start()
        forwards.append(onward)
    for copy in nears:
        copy.wait_recv()
    project(sibling)
    for chip in range(1, chips):
        project(lax.rem(me - 2 * chip + groups, groups))
    for onward in forwards:
        onward.wait_recv()
    for chip in range(1, chips):
        project(lax.rem(sibling - 2 * chip + groups, groups))

    for copy in deals + returns + [far[2] for far in fars] + nears + forwards:
        copy.wait_send()
    for hop in range(hops):

        @pl.when(has_next)
        def _(hop=hop):
            relay(hop).wait_send()


def on_device(
    queries, keys, values, out_gate, write_rate, log_decay, doc_starts, norm_gain, out_weight
):
    tokens, width = queries.shape
    heads_all = log_decay.shape[1]
    depth = width // heads_all
    groups = lax.axis_size("head")
    heads_here = heads_all // groups
    hops = lax.axis_size("seq") // 2
    steps = 2 * tokens
    sems = pltpu.SemaphoreType.DMA
    return pl.pallas_call(
        join_kernel,
        in_specs=[pl.BlockSpec(memory_space=pltpu.SMEM)]
        + [pl.BlockSpec(memory_space=pltpu.VMEM)] * 8,
        out_specs=pl.BlockSpec(memory_space=pltpu.VMEM),
        out_shape=jax.ShapeDtypeStruct((groups * tokens, out_weight.shape[1]), BF16),
        scratch_shapes=[
            pltpu.VMEM((tokens, width), F32),
            pltpu.VMEM((tokens, width), BF16),
            pltpu.VMEM((heads_all, 2, depth, depth), BF16),
            pltpu.VMEM((heads_all, steps, depth), BF16),
            pltpu.VMEM((heads_all, steps, depth), BF16),
            pltpu.VMEM((heads_all, 1, steps), F32),
            pltpu.VMEM((groups, heads_here, 2, depth, depth), BF16),
            pltpu.VMEM((hops, heads_here, depth, depth), BF16),
            pltpu.VMEM((hops, heads_here, depth, depth), BF16),
            pltpu.VMEM((groups, heads_here, depth, depth), BF16),
            pltpu.VMEM((groups, heads_here, depth, depth), BF16),
            pltpu.VMEM((groups, tokens, width), BF16),
            sems((groups,)),
            sems((groups,)),
            sems((hops,)),
            sems((hops,)),
            sems((groups,)),
            sems((groups,)),
            sems((groups, groups // 2)),
            sems((groups, groups // 2)),
            sems((groups, groups // 2)),
            sems((groups, groups // 2)),
        ],
        compiler_params=pltpu.CompilerParams(
            collective_id=0, has_side_effects=True, vmem_limit_bytes=40 * 1024 * 1024
        ),
        name="join",
    )(
        doc_starts,
        queries,
        keys.reshape(steps, width),
        values.reshape(steps, width),
        write_rate.reshape(steps, heads_all),
        log_decay,
        out_gate,
        norm_gain.reshape(1, depth),
        out_weight,
    )


def solution(mesh):
    placed = (
        P(("rep", "seq", "head"), None),
        P(("rep", "seq", "head"), None, None),
        P(("rep", "seq", "head"), None, None),
        P(("rep", "seq", "head"), None),
        P(("rep", "seq", "head"), None, None),
        P(("rep", "seq", "head"), None),
        P("rep"),
        P(),
        P(None, "head"),
    )
    return jax.shard_map(
        on_device, mesh=mesh, in_specs=placed, out_specs=P(("rep", "seq"), "head"), check_vma=False
    )
```

```python
import jax
import jax.numpy as jnp
from jax import lax
from jax.experimental import pallas as pl
from jax.experimental.pallas import tpu as pltpu
from jax.sharding import PartitionSpec as P

F32 = jnp.float32
BF16 = jnp.bfloat16


def mm(a, b):
    return jnp.dot(a.astype(BF16), b.astype(BF16), preferred_element_type=F32)


def mm_nt(a, b):
    return lax.dot_general(
        a.astype(BF16), b.astype(BF16), (((1,), (1,)), ((), ())), preferred_element_type=F32
    )


def mm_tn(a, b):
    return lax.dot_general(
        a.astype(BF16), b.astype(BF16), (((0,), (0,)), ((), ())), preferred_element_type=F32
    )


def iota(shape, dim):
    return lax.broadcasted_iota(jnp.int32, shape, dim)


def unit_lower_inverse(parts, half):
    rows, cols = iota((half, half), 0), iota((half, half), 1)
    size = 1
    inverses = None
    while size < half:
        row_block, col_block = rows // size, cols // size
        link = (row_block == col_block + 1) & (row_block % 2 == 1)
        linked = [jnp.where(link, part, 0.0) for part in parts]
        if inverses is None:
            eye = jnp.where(rows == cols, 1.0, 0.0)
            inverses = [eye - part for part in linked]
        else:
            short = [inverse.astype(BF16) for inverse in inverses]
            middle = [mm(part, inverse) for part, inverse in zip(linked, short)]
            fixes = [mm(inverse, part) for inverse, part in zip(short, middle)]
            inverses = [inverse - fix for inverse, fix in zip(inverses, fixes)]
        size *= 2
    return inverses


class Frame:
    def __init__(self, doc_ref, tokens, first):
        steps, half = 2 * tokens, tokens
        docs = doc_ref.shape[0]

        def doc_of(position):
            return sum((position >= doc_ref[index]).astype(jnp.int32) for index in range(docs))

        self.tokens, self.steps, self.half = tokens, steps, half
        self.doc_before = doc_of(first - 1)
        self.doc_last = doc_of(first + tokens - 1)
        self.step_doc_col = doc_of(first + iota((steps, half), 0) // 2)
        self.step_doc_row = doc_of(first + iota((1, steps), 1) // 2)
        self.token_doc_col = doc_of(first + iota((tokens, steps), 0))
        col_ids = iota((tokens, steps), 1)
        self.score_mask = (col_ids <= 2 * iota((tokens, steps), 0) + 1) & (
            self.token_doc_col == self.step_doc_row
        )
        self.step_tri = (iota((steps, tokens), 1) <= iota((steps, tokens), 0) // 2).astype(BF16)
        self.token_tri = (iota((tokens, tokens), 1) <= iota((tokens, tokens), 0)).astype(BF16)
        self.row_tri = (iota((tokens, steps), 0) <= iota((tokens, steps), 1) // 2).astype(BF16)
        rows, cols = iota((half, half), 0), iota((half, half), 1)
        self.eye = rows == cols
        lower = rows > cols
        self.docs_low = self.step_doc_col[half:] == self.step_doc_row[:, :half]
        self.docs_first = (self.step_doc_col[:half] == self.step_doc_row[:, :half]) & lower
        self.docs_second = (self.step_doc_col[half:] == self.step_doc_row[:, half:]) & lower
        woven, split = iota((steps, steps), 0), iota((steps, steps), 1)
        self.weave = (woven == 2 * (split % tokens) + split // tokens).astype(BF16)
        self.eye_steps = (iota((steps, steps), 0) == iota((steps, steps), 1)).astype(BF16)


def head_lanes(head, depth):
    return pl.ds(pl.multiple_of(head * depth, depth), depth)


def head_decay(frame, decay_ref, head, depth):
    pick = (iota((decay_ref.shape[0], depth), 0) == head).astype(BF16)
    decay_col = mm_tn(decay_ref[...], pick)
    return decay_col, mm_tn(decay_col, frame.row_tri)[:1]


def state_phase(frame, heads, key_ref, value_ref, rate_ref, decay_ref, keep, state_ref, depth):
    half, steps = frame.half, frame.steps
    parts, corners, work = [], [], []
    for head in heads:
        pick = (iota((decay_ref.shape[0], depth), 0) == head).astype(BF16)
        lanes = head_lanes(head, depth)
        key, value = key_ref[:, lanes], value_ref[:, lanes]
        rate_split = jnp.concatenate([mm_tn(rate_ref[0], pick), mm_tn(rate_ref[1], pick)], 0)
        rate_col = mm(frame.weave, rate_split)
        decay_col, total_row = head_decay(frame, decay_ref, head, depth)
        total_col = mm(frame.step_tri, decay_col)
        rate_row = mm_tn(rate_col, frame.eye_steps)[:1]
        key_one, key_two = key[:half], key[half:]
        gram_one, gram_two = mm_nt(key_one, key_one), mm_nt(key_two, key_two)
        gram_low = mm_nt(key_two, key_one)
        diag_one = jnp.where(frame.eye, gram_one, 0.0)
        diag_two = jnp.where(frame.eye, gram_two, 0.0)
        inv_row = lax.rsqrt(
            jnp.concatenate(
                [jnp.sum(diag_one, 0, keepdims=True), jnp.sum(diag_two, 0, keepdims=True)], 1
            )
            + 1e-06
        )
        inv_col = lax.rsqrt(
            jnp.concatenate(
                [jnp.sum(diag_one, 1, keepdims=True), jnp.sum(diag_two, 1, keepdims=True)], 0
            )
            + 1e-06
        )
        left = rate_col * inv_col

        def linked(gram, mask, rows, cols):
            ratio = jnp.exp(jnp.minimum(total_col[rows] - total_row[:, cols], 0.0))
            return jnp.where(mask, gram * left[rows] * inv_row[:, cols] * ratio, 0.0)

        upper, lower = slice(0, half), slice(half, steps)
        parts.append(linked(gram_one, frame.docs_first, upper, upper))
        parts.append(linked(gram_two, frame.docs_second, lower, lower))
        corners.append(linked(gram_low, frame.docs_low, lower, upper))
        work.append((key, value, total_col, total_row, rate_row, inv_row, inv_col))

    inverses = unit_lower_inverse(parts, half)
    for local, head in enumerate(heads):
        key, value, total_col, total_row, rate_row, inv_row, inv_col = work[local]
        inv_one, inv_two = inverses[2 * local], inverses[2 * local + 1]
        inv_low = -mm(inv_two, mm(corners[local], inv_one))
        start_row = jnp.where(
            frame.step_doc_row == frame.doc_before, jnp.exp(total_row), 0.0
        )
        last = total_col[steps - 1 :]
        end_col = inv_col * jnp.where(
            frame.step_doc_col == frame.doc_last, jnp.exp(last - total_col), 0.0
        )

        def solve(scale, right):
            first_rows = mm(inv_one * scale[:, :half], right[:half])
            left = jnp.concatenate([inv_low * scale[:, :half], inv_two * scale[:, half:]], 1)
            return jnp.concatenate([first_rows, mm(left, right)], 0)

        written = solve(rate_row, value)
        erased = solve(rate_row * start_row * inv_row, key)
        last_gain = jnp.where(frame.doc_last == frame.doc_before, jnp.exp(last), 0.0)
        state_ref[head, 0] = (
            jnp.where(frame.eye, last_gain, 0.0) - mm_tn(key, erased * end_col)
        ).astype(BF16)
        state_ref[head, 1] = mm_tn(key, written * end_col).astype(BF16)
        written_ref, erased_ref, inverse_ref = keep
        written_ref[head] = written.astype(BF16)
        erased_ref[head] = erased.astype(BF16)
        inverse_ref[head] = inv_row


def read_phase(frame, head, query_ref, key_ref, decay_ref, keep, inner_ref, carried_ref, depth):
    written_ref, erased_ref, inverse_ref = keep
    lanes = head_lanes(head, depth)
    query, key = query_ref[:, lanes], key_ref[:, lanes]
    decay_col, total_row = head_decay(frame, decay_ref, head, depth)
    token_col = mm(frame.token_tri, decay_col)
    token_wide = jnp.concatenate([token_col, token_col], 1)
    start_token = jnp.where(
        frame.token_doc_col[:, : frame.half] == frame.doc_before, jnp.exp(token_col), 0.0
    )
    ratio = jnp.exp(jnp.minimum(token_wide - total_row, 0.0))
    scores = jnp.where(frame.score_mask, mm_nt(query, key) * inverse_ref[head] * ratio, 0.0)
    scores = scores.astype(BF16)
    inner_ref[:, lanes] = mm(scores, written_ref[head])
    carried_ref[:, lanes] = (
        start_token * query.astype(F32) - mm(scores, erased_ref[head])
    ).astype(carried_ref.dtype)


MESH = pl.DeviceIdType.MESH


def join_kernel(
    doc_ref,
    query_ref,
    key_ref,
    value_ref,
    rate_ref,
    decay_ref,
    gate_hbm,
    gain_ref,
    weight_hbm,
    out_ref,
    gate_ref,
    weight_ref,
    load_sems,
    inner_ref,
    carried_ref,
    state_ref,
    written_ref,
    erased_ref,
    inverse_ref,
    mine,
    relay_out,
    relay_in,
    starts,
    back,
    normed,
    deal_send,
    deal_recv,
    relay_send,
    relay_recv,
    back_send,
    back_recv,
    far_send,
    far_recv,
    near_send,
    near_recv,
):
    groups, heads_here, _, depth, _ = mine.shape
    hops = relay_in.shape[0]
    heads_all = groups * heads_here
    tokens = query_ref.shape[0]
    block = heads_here * depth
    me, place, places = lax.axis_index("head"), lax.axis_index("seq"), lax.axis_size("seq")
    has_next, has_prior = place < places - 1, place > 0
    chips = groups // 2
    sibling = me + 1 - 2 * lax.rem(me, 2)

    def to_head(source, target, send, recv, peer):
        return pltpu.make_async_remote_copy(
            src_ref=source,
            dst_ref=target,
            send_sem=send,
            recv_sem=recv,
            device_id={"head": peer},
            device_id_type=MESH,
        )

    weight_load = pltpu.make_async_copy(weight_hbm, weight_ref, load_sems.at[0])
    gate_load = pltpu.make_async_copy(gate_hbm, gate_ref, load_sems.at[1])
    weight_load.start()
    gate_load.start()
    barrier = pltpu.get_barrier_semaphore()
    for offset in range(1, groups):
        pl.semaphore_signal(
            barrier, inc=1, device_id={"head": lax.rem(me + offset, groups)}, device_id_type=MESH
        )

    @pl.when(has_next)
    def _():
        pl.semaphore_signal(barrier, inc=1, device_id={"seq": place + 1}, device_id_type=MESH)

    @pl.when(has_prior)
    def _():
        pl.semaphore_signal(barrier, inc=1, device_id={"seq": place - 1}, device_id_type=MESH)

    @pl.when(place == 0)
    def _():
        relay_in[...] = jnp.zeros_like(relay_in)

    frame = Frame(doc_ref, tokens, (place * groups + me) * tokens)
    keep = (written_ref, erased_ref, inverse_ref)
    order = []
    for chip in range(1, chips):
        order += [lax.rem(me + 2 * chip, groups), lax.rem(sibling + 2 * chip, groups)]
    order += [sibling, me]
    together = max(1, 4 // heads_here)
    deals = []
    for begin in range(0, groups, together):
        batch = list(range(begin, min(begin + together, groups)))
        heads = [order[spot] * heads_here + local for spot in batch for local in range(heads_here)]
        state_phase(
            frame, heads, key_ref, value_ref, rate_ref, decay_ref, keep, state_ref, depth
        )
        if begin == 0:
            pl.semaphore_wait(
                barrier, groups - 1 + has_next.astype(jnp.int32) + has_prior.astype(jnp.int32)
            )
        for spot in batch:
            if spot == groups - 1:
                continue
            copy = to_head(
                state_ref.at[pl.ds(order[spot] * heads_here, heads_here)],
                mine.at[me],
                deal_send.at[spot],
                deal_recv.at[spot],
                order[spot],
            )
            copy.start()
            deals.append(copy)
    mine[me] = state_ref[pl.ds(me * heads_here, heads_here)]

    for copy in deals:
        copy.wait_recv()

    sums, maps = [], []
    for local in range(heads_here):
        chain = [None, mine[0, local, 1].astype(F32)]
        for index in range(1, groups):
            chain.append(
                mm(mine[index, local, 0], chain[-1]) + mine[index, local, 1].astype(F32)
            )
        sums.append(chain)

    def relay(hop):
        return pltpu.make_async_remote_copy(
            src_ref=relay_out.at[hop],
            dst_ref=relay_in.at[hop],
            send_sem=relay_send.at[hop],
            recv_sem=relay_recv.at[hop],
            device_id={"seq": place + 1},
            device_id_type=MESH,
        )

    for hop in range(hops):
        for local in range(heads_here):
            value = sums[local][groups]
            if hop:
                value = value + mm(maps[local][groups], relay_in[hop - 1, local])
            relay_out[hop, local] = value.astype(BF16)

        @pl.when(has_next)
        def _(hop=hop):
            relay(hop).start()

        if hop == 0:
            for local in range(heads_here):
                chain = [None, mine[0, local, 0]]
                for index in range(1, groups):
                    chain.append(mm(mine[index, local, 0], chain[-1]).astype(BF16))
                maps.append(chain)

        for head in range(heads_all * hop // hops, heads_all * (hop + 1) // hops):
            read_phase(
                frame, head, query_ref, key_ref, decay_ref, keep, inner_ref, carried_ref, depth
            )

        @pl.when(has_prior)
        def _(hop=hop):
            relay(hop).wait_recv()

    for local in range(heads_here):
        incoming = relay_in[hops - 1, local]
        starts[0, local] = incoming
        for index in range(1, groups):
            starts[index, local] = (
                mm(maps[local][index], incoming) + sums[local][index]
            ).astype(BF16)
    returns = []
    for spot in range(groups - 1):
        copy = to_head(
            starts.at[order[spot]], back.at[me], back_send.at[spot], back_recv.at[spot], order[spot]
        )
        copy.start()
        returns.append(copy)
    back[me] = starts[me]

    gate_load.wait()
    gain = gain_ref[...]
    fars, nears = [], []
    spots = [groups - 1, groups - 2, *range(groups - 2)]

    def owner_of(device, piece):
        spot = spots[piece]
        other = device + 1 - 2 * lax.rem(device, 2)
        base = other if spot == groups - 2 or (spot < groups - 2 and spot % 2) else device
        shift = 0 if spot >= groups - 2 else 2 * (spot // 2 + 1)
        return lax.rem(base - shift + groups, groups)

    for piece in range(groups):
        if piece:
            returns[spots[piece]].wait_recv()
        owner = owner_of(me, piece)
        for local in range(heads_here):
            lanes = pl.ds(pl.multiple_of(owner * block + local * depth, depth), depth)
            readout = inner_ref[:, lanes] + mm(carried_ref[:, lanes], back[owner, local])
            gate = gate_ref[:, lanes].astype(F32)
            inv_rms = lax.rsqrt(jnp.mean(readout * readout, -1, keepdims=True) + 1e-05)
            normed[me, :, lanes] = (
                readout * inv_rms * gain * (gate / (1.0 + jnp.exp(-gate)))
            ).astype(BF16)
        lanes = pl.ds(pl.multiple_of(owner * block, block), block)
        here = normed.at[me, :, lanes]
        for chip in range(1, chips):
            copy = to_head(
                here,
                here,
                far_send.at[piece, chip],
                far_recv.at[piece, chip],
                lax.rem(me + 2 * chip, groups),
            )
            copy.start()
            fars.append((chip, piece, copy))
        copy = to_head(here, here, near_send.at[piece, 0], near_recv.at[piece, 0], sibling)
        copy.start()
        nears.append(copy)

    def project(source):
        rows = pl.ds(pl.multiple_of(source * tokens, tokens), tokens)
        out_ref[rows, :] = jnp.dot(
            normed[source], weight_ref[...], preferred_element_type=F32
        ).astype(out_ref.dtype)

    weight_load.wait()
    project(me)
    forwards = []
    for chip, piece, copy in fars:
        source = lax.rem(me - 2 * chip + groups, groups)
        owner = owner_of(source, piece)
        there = normed.at[source, :, pl.ds(pl.multiple_of(owner * block, block), block)]
        copy.wait_recv()
        onward = to_head(
            there, there, near_send.at[piece, chip], near_recv.at[piece, chip], sibling
        )
        onward.start()
        forwards.append(onward)
    for copy in nears:
        copy.wait_recv()
    project(sibling)
    for chip in range(1, chips):
        project(lax.rem(me - 2 * chip + groups, groups))
    for onward in forwards:
        onward.wait_recv()
    for chip in range(1, chips):
        project(lax.rem(sibling - 2 * chip + groups, groups))

    for copy in deals + returns + [far[2] for far in fars] + nears + forwards:
        copy.wait_send()
    for hop in range(hops):

        @pl.when(has_next)
        def _(hop=hop):
            relay(hop).wait_send()


def on_device(
    queries, keys, values, out_gate, write_rate, log_decay, doc_starts, norm_gain, out_weight
):
    tokens, width = queries.shape
    heads_all = log_decay.shape[1]
    depth = width // heads_all
    groups = lax.axis_size("head")
    heads_here = heads_all // groups
    hops = lax.axis_size("seq") // 2
    steps = 2 * tokens
    sems = pltpu.SemaphoreType.DMA
    return pl.pallas_call(
        join_kernel,
        in_specs=[pl.BlockSpec(memory_space=pltpu.SMEM)]
        + [pl.BlockSpec(memory_space=pltpu.VMEM)] * 5
        + [
            pl.BlockSpec(memory_space=pltpu.HBM),
            pl.BlockSpec(memory_space=pltpu.VMEM),
            pl.BlockSpec(memory_space=pltpu.HBM),
        ],
        out_specs=pl.BlockSpec(memory_space=pltpu.VMEM),
        out_shape=jax.ShapeDtypeStruct((groups * tokens, out_weight.shape[1]), BF16),
        scratch_shapes=[
            pltpu.VMEM(out_gate.shape, BF16),
            pltpu.VMEM(out_weight.shape, BF16),
            sems((2,)),
            pltpu.VMEM((tokens, width), F32),
            pltpu.VMEM((tokens, width), BF16),
            pltpu.VMEM((heads_all, 2, depth, depth), BF16),
            pltpu.VMEM((heads_all, steps, depth), BF16),
            pltpu.VMEM((heads_all, steps, depth), BF16),
            pltpu.VMEM((heads_all, 1, steps), F32),
            pltpu.VMEM((groups, heads_here, 2, depth, depth), BF16),
            pltpu.VMEM((hops, heads_here, depth, depth), BF16),
            pltpu.VMEM((hops, heads_here, depth, depth), BF16),
            pltpu.VMEM((groups, heads_here, depth, depth), BF16),
            pltpu.VMEM((groups, heads_here, depth, depth), BF16),
            pltpu.VMEM((groups, tokens, width), BF16),
            sems((groups,)),
            sems((groups,)),
            sems((hops,)),
            sems((hops,)),
            sems((groups,)),
            sems((groups,)),
            sems((groups, groups // 2)),
            sems((groups, groups // 2)),
            sems((groups, groups // 2)),
            sems((groups, groups // 2)),
        ],
        compiler_params=pltpu.CompilerParams(
            collective_id=0, has_side_effects=True, vmem_limit_bytes=40 * 1024 * 1024
        ),
        name="join",
    )(
        doc_starts,
        queries,
        keys.reshape(steps, width),
        values.reshape(steps, width),
        write_rate.transpose(1, 2, 0),
        log_decay.T,
        out_gate,
        norm_gain.reshape(1, depth),
        out_weight,
    )


def solution(mesh):
    placed = (
        P(("rep", "seq", "head"), None),
        P(("rep", "seq", "head"), None, None),
        P(("rep", "seq", "head"), None, None),
        P(("rep", "seq", "head"), None),
        P(("rep", "seq", "head"), None, None),
        P(("rep", "seq", "head"), None),
        P("rep"),
        P(),
        P(None, "head"),
    )
    return jax.shard_map(
        on_device, mesh=mesh, in_specs=placed, out_specs=P(("rep", "seq"), "head"), check_vma=False
    )
```

```python
import jax
import jax.numpy as jnp
from jax import lax
from jax.experimental import pallas as pl
from jax.experimental.pallas import tpu as pltpu
from jax.sharding import PartitionSpec as P

F32 = jnp.float32
BF16 = jnp.bfloat16


def mm(a, b):
    return jnp.dot(a.astype(BF16), b.astype(BF16), preferred_element_type=F32)


def mm_nt(a, b):
    return lax.dot_general(
        a.astype(BF16), b.astype(BF16), (((1,), (1,)), ((), ())), preferred_element_type=F32
    )


def mm_tn(a, b):
    return lax.dot_general(
        a.astype(BF16), b.astype(BF16), (((0,), (0,)), ((), ())), preferred_element_type=F32
    )


def iota(shape, dim):
    return lax.broadcasted_iota(jnp.int32, shape, dim)


def unit_lower_inverse(parts, half):
    rows, cols = iota((half, half), 0), iota((half, half), 1)
    size = 1
    inverses = None
    while size < half:
        row_block, col_block = rows // size, cols // size
        link = (row_block == col_block + 1) & (row_block % 2 == 1)
        linked = [jnp.where(link, part, 0.0) for part in parts]
        if inverses is None:
            eye = jnp.where(rows == cols, 1.0, 0.0)
            inverses = [eye - part for part in linked]
        else:
            short = [inverse.astype(BF16) for inverse in inverses]
            middle = [mm(part, inverse) for part, inverse in zip(linked, short)]
            fixes = [mm(inverse, part) for inverse, part in zip(short, middle)]
            inverses = [inverse - fix for inverse, fix in zip(inverses, fixes)]
        size *= 2
    return inverses


class Frame:
    def __init__(self, doc_ref, tokens, first):
        steps, half = 2 * tokens, tokens
        docs = doc_ref.shape[0]

        def doc_of(position):
            return sum((position >= doc_ref[index]).astype(jnp.int32) for index in range(docs))

        self.tokens, self.steps, self.half = tokens, steps, half
        self.doc_before = doc_of(first - 1)
        self.doc_last = doc_of(first + tokens - 1)
        self.step_doc_col = doc_of(first + iota((steps, half), 0) // 2)
        self.step_doc_row = doc_of(first + iota((1, steps), 1) // 2)
        self.token_doc_col = doc_of(first + iota((tokens, steps), 0))
        col_ids = iota((tokens, steps), 1)
        self.score_mask = (col_ids <= 2 * iota((tokens, steps), 0) + 1) & (
            self.token_doc_col == self.step_doc_row
        )
        self.step_tri = (iota((steps, tokens), 1) <= iota((steps, tokens), 0) // 2).astype(BF16)
        self.token_tri = (iota((tokens, tokens), 1) <= iota((tokens, tokens), 0)).astype(BF16)
        self.row_tri = (iota((tokens, steps), 0) <= iota((tokens, steps), 1) // 2).astype(BF16)
        rows, cols = iota((half, half), 0), iota((half, half), 1)
        self.eye = rows == cols
        lower = rows > cols
        self.docs_low = self.step_doc_col[half:] == self.step_doc_row[:, :half]
        self.docs_first = (self.step_doc_col[:half] == self.step_doc_row[:, :half]) & lower
        self.docs_second = (self.step_doc_col[half:] == self.step_doc_row[:, half:]) & lower
        self.eye_steps = (iota((steps, steps), 0) == iota((steps, steps), 1)).astype(BF16)


def head_lanes(head, depth):
    return pl.ds(pl.multiple_of(head * depth, depth), depth)


def head_decay(frame, decay_ref, head, depth):
    pick = (iota((decay_ref.shape[1], depth), 0) == head).astype(BF16)
    decay_col = mm(decay_ref[...], pick)
    return decay_col, mm_tn(decay_col, frame.row_tri)[:1]


def state_phase(frame, heads, key_ref, value_ref, rate_ref, decay_ref, keep, state_ref, depth):
    half, steps = frame.half, frame.steps
    parts, corners, work = [], [], []
    for head in heads:
        pick = (iota((rate_ref.shape[1], depth), 0) == head).astype(BF16)
        lanes = head_lanes(head, depth)
        key, value = key_ref[:, lanes], value_ref[:, lanes]
        rate_col = mm(rate_ref[...], pick)
        decay_col, total_row = head_decay(frame, decay_ref, head, depth)
        total_col = mm(frame.step_tri, decay_col)
        rate_row = mm_tn(rate_col, frame.eye_steps)[:1]
        key_one, key_two = key[:half], key[half:]
        gram_one, gram_two = mm_nt(key_one, key_one), mm_nt(key_two, key_two)
        gram_low = mm_nt(key_two, key_one)
        diag_one = jnp.where(frame.eye, gram_one, 0.0)
        diag_two = jnp.where(frame.eye, gram_two, 0.0)
        inv_row = lax.rsqrt(
            jnp.concatenate(
                [jnp.sum(diag_one, 0, keepdims=True), jnp.sum(diag_two, 0, keepdims=True)], 1
            )
            + 1e-06
        )
        inv_col = lax.rsqrt(
            jnp.concatenate(
                [jnp.sum(diag_one, 1, keepdims=True), jnp.sum(diag_two, 1, keepdims=True)], 0
            )
            + 1e-06
        )
        left = rate_col * inv_col

        def linked(gram, mask, rows, cols):
            ratio = jnp.exp(jnp.minimum(total_col[rows] - total_row[:, cols], 0.0))
            return jnp.where(mask, gram * left[rows] * inv_row[:, cols] * ratio, 0.0)

        upper, lower = slice(0, half), slice(half, steps)
        parts.append(linked(gram_one, frame.docs_first, upper, upper))
        parts.append(linked(gram_two, frame.docs_second, lower, lower))
        corners.append(linked(gram_low, frame.docs_low, lower, upper))
        work.append((key, value, total_col, total_row, rate_row, inv_row, inv_col))

    inverses = unit_lower_inverse(parts, half)
    for local, head in enumerate(heads):
        key, value, total_col, total_row, rate_row, inv_row, inv_col = work[local]
        inv_one, inv_two = inverses[2 * local], inverses[2 * local + 1]
        inv_low = -mm(inv_two, mm(corners[local], inv_one))
        start_row = jnp.where(
            frame.step_doc_row == frame.doc_before, jnp.exp(total_row), 0.0
        )
        last = total_col[steps - 1 :]
        end_col = inv_col * jnp.where(
            frame.step_doc_col == frame.doc_last, jnp.exp(last - total_col), 0.0
        )

        def solve(scale, right):
            first_rows = mm(inv_one * scale[:, :half], right[:half])
            left = jnp.concatenate([inv_low * scale[:, :half], inv_two * scale[:, half:]], 1)
            return jnp.concatenate([first_rows, mm(left, right)], 0)

        written = solve(rate_row, value)
        erased = solve(rate_row * start_row * inv_row, key)
        last_gain = jnp.where(frame.doc_last == frame.doc_before, jnp.exp(last), 0.0)
        state_ref[head, 0] = (
            jnp.where(frame.eye, last_gain, 0.0) - mm_tn(key, erased * end_col)
        ).astype(BF16)
        state_ref[head, 1] = mm_tn(key, written * end_col).astype(BF16)
        written_ref, erased_ref, inverse_ref = keep
        written_ref[head] = written.astype(BF16)
        erased_ref[head] = erased.astype(BF16)
        inverse_ref[head] = inv_row


def read_phase(frame, head, query_ref, key_ref, decay_ref, keep, inner_ref, carried_ref, depth):
    written_ref, erased_ref, inverse_ref = keep
    lanes = head_lanes(head, depth)
    query, key = query_ref[:, lanes], key_ref[:, lanes]
    decay_col, total_row = head_decay(frame, decay_ref, head, depth)
    token_col = mm(frame.token_tri, decay_col)
    token_wide = jnp.concatenate([token_col, token_col], 1)
    start_token = jnp.where(
        frame.token_doc_col[:, : frame.half] == frame.doc_before, jnp.exp(token_col), 0.0
    )
    ratio = jnp.exp(jnp.minimum(token_wide - total_row, 0.0))
    scores = jnp.where(frame.score_mask, mm_nt(query, key) * inverse_ref[head] * ratio, 0.0)
    scores = scores.astype(BF16)
    inner_ref[:, lanes] = mm(scores, written_ref[head])
    carried_ref[:, lanes] = (
        start_token * query.astype(F32) - mm(scores, erased_ref[head])
    ).astype(carried_ref.dtype)


MESH = pl.DeviceIdType.MESH


def join_kernel(
    doc_ref,
    query_ref,
    key_ref,
    value_ref,
    rate_ref,
    decay_ref,
    gate_ref,
    gain_ref,
    weight_ref,
    out_ref,
    inner_ref,
    carried_ref,
    state_ref,
    written_ref,
    erased_ref,
    inverse_ref,
    mine,
    relay_out,
    relay_in,
    starts,
    back,
    normed,
    deal_send,
    deal_recv,
    relay_send,
    relay_recv,
    back_send,
    back_recv,
    far_send,
    far_recv,
    near_send,
    near_recv,
):
    groups, heads_here, _, depth, _ = mine.shape
    hops = relay_in.shape[0]
    heads_all = groups * heads_here
    tokens = query_ref.shape[0]
    block = heads_here * depth
    me, place, places = lax.axis_index("head"), lax.axis_index("seq"), lax.axis_size("seq")
    has_next, has_prior = place < places - 1, place > 0
    chips = groups // 2
    sibling = me + 1 - 2 * lax.rem(me, 2)

    def to_head(source, target, send, recv, peer):
        return pltpu.make_async_remote_copy(
            src_ref=source,
            dst_ref=target,
            send_sem=send,
            recv_sem=recv,
            device_id={"head": peer},
            device_id_type=MESH,
        )

    barrier = pltpu.get_barrier_semaphore()
    for offset in range(1, groups):
        pl.semaphore_signal(
            barrier, inc=1, device_id={"head": lax.rem(me + offset, groups)}, device_id_type=MESH
        )

    @pl.when(has_next)
    def _():
        pl.semaphore_signal(barrier, inc=1, device_id={"seq": place + 1}, device_id_type=MESH)

    @pl.when(has_prior)
    def _():
        pl.semaphore_signal(barrier, inc=1, device_id={"seq": place - 1}, device_id_type=MESH)

    @pl.when(place == 0)
    def _():
        relay_in[...] = jnp.zeros_like(relay_in)

    frame = Frame(doc_ref, tokens, (place * groups + me) * tokens)
    keep = (written_ref, erased_ref, inverse_ref)
    order = []
    for chip in range(1, chips):
        order += [lax.rem(me + 2 * chip, groups), lax.rem(sibling + 2 * chip, groups)]
    order += [sibling, me]
    together = max(1, 4 // heads_here)
    deals = []
    for begin in range(0, groups, together):
        batch = list(range(begin, min(begin + together, groups)))
        heads = [order[spot] * heads_here + local for spot in batch for local in range(heads_here)]
        state_phase(
            frame, heads, key_ref, value_ref, rate_ref, decay_ref, keep, state_ref, depth
        )
        if begin == 0:
            pl.semaphore_wait(
                barrier, groups - 1 + has_next.astype(jnp.int32) + has_prior.astype(jnp.int32)
            )
        for spot in batch:
            if spot == groups - 1:
                continue
            copy = to_head(
                state_ref.at[pl.ds(order[spot] * heads_here, heads_here)],
                mine.at[me],
                deal_send.at[spot],
                deal_recv.at[spot],
                order[spot],
            )
            copy.start()
            deals.append(copy)
    mine[me] = state_ref[pl.ds(me * heads_here, heads_here)]

    for copy in deals:
        copy.wait_recv()

    sums, maps = [], []
    for local in range(heads_here):
        chain = [None, mine[0, local, 1].astype(F32)]
        for index in range(1, groups):
            chain.append(
                mm(mine[index, local, 0], chain[-1]) + mine[index, local, 1].astype(F32)
            )
        sums.append(chain)

    def relay(hop):
        return pltpu.make_async_remote_copy(
            src_ref=relay_out.at[hop],
            dst_ref=relay_in.at[hop],
            send_sem=relay_send.at[hop],
            recv_sem=relay_recv.at[hop],
            device_id={"seq": place + 1},
            device_id_type=MESH,
        )

    for hop in range(hops):
        for local in range(heads_here):
            value = sums[local][groups]
            if hop:
                value = value + mm(maps[local][groups], relay_in[hop - 1, local])
            relay_out[hop, local] = value.astype(BF16)

        @pl.when(has_next)
        def _(hop=hop):
            relay(hop).start()

        if hop == 0:
            for local in range(heads_here):
                chain = [None, mine[0, local, 0]]
                for index in range(1, groups):
                    chain.append(mm(mine[index, local, 0], chain[-1]).astype(BF16))
                maps.append(chain)

        for head in range(heads_all * hop // hops, heads_all * (hop + 1) // hops):
            read_phase(
                frame, head, query_ref, key_ref, decay_ref, keep, inner_ref, carried_ref, depth
            )

        @pl.when(has_prior)
        def _(hop=hop):
            relay(hop).wait_recv()

    for local in range(heads_here):
        incoming = relay_in[hops - 1, local]
        starts[0, local] = incoming
        for index in range(1, groups):
            starts[index, local] = (
                mm(maps[local][index], incoming) + sums[local][index]
            ).astype(BF16)
    returns = []
    for spot in range(groups - 1):
        copy = to_head(
            starts.at[order[spot]], back.at[me], back_send.at[spot], back_recv.at[spot], order[spot]
        )
        copy.start()
        returns.append(copy)
    back[me] = starts[me]

    gain = gain_ref[...]
    fars, nears = [], []
    spots = [groups - 1, groups - 2, *range(groups - 2)]

    def owner_of(device, piece):
        spot = spots[piece]
        other = device + 1 - 2 * lax.rem(device, 2)
        base = other if spot == groups - 2 or (spot < groups - 2 and spot % 2) else device
        shift = 0 if spot >= groups - 2 else 2 * (spot // 2 + 1)
        return lax.rem(base - shift + groups, groups)

    for piece in range(groups):
        if piece:
            returns[spots[piece]].wait_recv()
        owner = owner_of(me, piece)
        for local in range(heads_here):
            lanes = pl.ds(pl.multiple_of(owner * block + local * depth, depth), depth)
            readout = inner_ref[:, lanes] + mm(carried_ref[:, lanes], back[owner, local])
            gate = gate_ref[:, lanes].astype(F32)
            inv_rms = lax.rsqrt(jnp.mean(readout * readout, -1, keepdims=True) + 1e-05)
            normed[me, :, lanes] = (
                readout * inv_rms * gain * (gate / (1.0 + jnp.exp(-gate)))
            ).astype(BF16)
        lanes = pl.ds(pl.multiple_of(owner * block, block), block)
        here = normed.at[me, :, lanes]
        for chip in range(1, chips):
            copy = to_head(
                here,
                here,
                far_send.at[piece, chip],
                far_recv.at[piece, chip],
                lax.rem(me + 2 * chip, groups),
            )
            copy.start()
            fars.append((chip, piece, copy))
        copy = to_head(here, here, near_send.at[piece, 0], near_recv.at[piece, 0], sibling)
        copy.start()
        nears.append(copy)

    def project(source):
        rows = pl.ds(pl.multiple_of(source * tokens, tokens), tokens)
        out_ref[rows, :] = jnp.dot(
            normed[source], weight_ref[...], preferred_element_type=F32
        ).astype(out_ref.dtype)

    project(me)
    forwards = []
    for chip, piece, copy in fars:
        source = lax.rem(me - 2 * chip + groups, groups)
        owner = owner_of(source, piece)
        there = normed.at[source, :, pl.ds(pl.multiple_of(owner * block, block), block)]
        copy.wait_recv()
        onward = to_head(
            there, there, near_send.at[piece, chip], near_recv.at[piece, chip], sibling
        )
        onward.start()
        forwards.append(onward)
    for copy in nears:
        copy.wait_recv()
    project(sibling)
    for chip in range(1, chips):
        project(lax.rem(me - 2 * chip + groups, groups))
    for onward in forwards:
        onward.wait_recv()
    for chip in range(1, chips):
        project(lax.rem(sibling - 2 * chip + groups, groups))

    for copy in deals + returns + [far[2] for far in fars] + nears + forwards:
        copy.wait_send()
    for hop in range(hops):

        @pl.when(has_next)
        def _(hop=hop):
            relay(hop).wait_send()


def on_device(
    queries, keys, values, out_gate, write_rate, log_decay, doc_starts, norm_gain, out_weight
):
    tokens, width = queries.shape
    heads_all = log_decay.shape[1]
    depth = width // heads_all
    groups = lax.axis_size("head")
    heads_here = heads_all // groups
    hops = lax.axis_size("seq") // 2
    steps = 2 * tokens
    sems = pltpu.SemaphoreType.DMA
    return pl.pallas_call(
        join_kernel,
        in_specs=[pl.BlockSpec(memory_space=pltpu.SMEM)]
        + [pl.BlockSpec(memory_space=pltpu.VMEM)] * 8,
        out_specs=pl.BlockSpec(memory_space=pltpu.VMEM),
        out_shape=jax.ShapeDtypeStruct((groups * tokens, out_weight.shape[1]), BF16),
        scratch_shapes=[
            pltpu.VMEM((tokens, width), F32),
            pltpu.VMEM((tokens, width), BF16),
            pltpu.VMEM((heads_all, 2, depth, depth), BF16),
            pltpu.VMEM((heads_all, steps, depth), BF16),
            pltpu.VMEM((heads_all, steps, depth), BF16),
            pltpu.VMEM((heads_all, 1, steps), F32),
            pltpu.VMEM((groups, heads_here, 2, depth, depth), BF16),
            pltpu.VMEM((hops, heads_here, depth, depth), BF16),
            pltpu.VMEM((hops, heads_here, depth, depth), BF16),
            pltpu.VMEM((groups, heads_here, depth, depth), BF16),
            pltpu.VMEM((groups, heads_here, depth, depth), BF16),
            pltpu.VMEM((groups, tokens, width), BF16),
            sems((groups,)),
            sems((groups,)),
            sems((hops,)),
            sems((hops,)),
            sems((groups,)),
            sems((groups,)),
            sems((groups, groups // 2)),
            sems((groups, groups // 2)),
            sems((groups, groups // 2)),
            sems((groups, groups // 2)),
        ],
        compiler_params=pltpu.CompilerParams(
            collective_id=0, has_side_effects=True, vmem_limit_bytes=40 * 1024 * 1024
        ),
        name="join",
    )(
        doc_starts,
        queries,
        keys.reshape(steps, width),
        values.reshape(steps, width),
        write_rate.reshape(steps, heads_all),
        log_decay,
        out_gate,
        norm_gain.reshape(1, depth),
        out_weight,
    )


def solution(mesh):
    placed = (
        P(("rep", "seq", "head"), None),
        P(("rep", "seq", "head"), None, None),
        P(("rep", "seq", "head"), None, None),
        P(("rep", "seq", "head"), None),
        P(("rep", "seq", "head"), None, None),
        P(("rep", "seq", "head"), None),
        P("rep"),
        P(),
        P(None, "head"),
    )
    return jax.shard_map(
        on_device, mesh=mesh, in_specs=placed, out_specs=P(("rep", "seq"), "head"), check_vma=False
    )
```
